32 devices in a mesh: grid: 4 (over x, core), proc: 8 (over z, y).
Axes of the slice: x: 2, y: 2, z: 4, core: 2. Of those that a mesh axis runs over, the one named last changes fastest.
Arguments:
- rhs: float32 [3, 4, 8, 256, 1024], P(None, 'grid', 'proc'), may hold values from -6 to 6
- tile_pairs: int32 [2, 4, 8, 16], P(None, 'grid', 'proc'), may hold values from -1 to 15, as said below
- tiles: bfloat16 [2, 4, 8, 16, 256, 256], P(None, 'grid', 'proc'), may hold values from -0.125 to 0.125
- dinv: float32 [3, 4, 8, 256, 256], P(None, 'grid', 'proc'), as said below
Outputs:
- solution: float32 [3, 4, 8, 256, 1024], P(None, 'grid', 'proc')
The draws below stay inside these ranges and needn't reach their ends.
Inputs may be any that keep to these rules, and one draw needn't show every extreme that they name: tile_pairs[t, g, p] holds distinct pair numbers in its first slots and -1 in the others; pair number q names block column q mod 8 and destination q // 8 (0: the same grid, 1: the partner grid). In every transition and grid one device uses all 16 slots and the others use 2 to 8 of them. Each dinv tile is lower triangular with diagonal entries between 0.5 and 1.4.
All inputs are finite; a program needn't handle non-finite values.
Results may differ from the reference program's by a relative error of at most 0.0021.
Values may be sent and summed in bfloat16 or wider, within the bound.
A program may use at most 128 MiB of HBM per device.

```python
import math
import jax
import jax.numpy as jnp
import numpy as np
from jax import lax

TILE = 256
RHS = 1024
LEVELS = 3
GRIDS = 4
PROCS = 8
CAP = 16
TRANS = 2


def draw_tile_pairs(key, part):
    row_total = TRANS * GRIDS * PROCS
    key_list = jax.random.split(jax.random.fold_in(key, 11), row_total)
    orders = jax.vmap(lambda single: jax.random.permutation(single, CAP))(key_list)
    orders = orders.reshape(TRANS, GRIDS, PROCS, CAP).astype(jnp.int32)
    counts = jax.random.randint(jax.random.fold_in(key, 12), (TRANS, GRIDS, PROCS), 2, CAP // 2 + 1)
    fullest = jax.random.randint(jax.random.fold_in(key, 13), (TRANS, GRIDS, 1), 0, PROCS)
    device_rank = lax.broadcasted_iota(jnp.int32, (TRANS, GRIDS, PROCS), 2)
    counts = jnp.where(device_rank == fullest, CAP, counts)
    slot_index = lax.broadcasted_iota(jnp.int32, (TRANS, GRIDS, PROCS, CAP), 3)
    return jnp.where(slot_index < counts[..., None], orders, -1).astype(jnp.int32)


def draw_dinv(key, part):
    first_key = jax.random.fold_in(key, 21)
    second_key = jax.random.fold_in(key, 22)
    full_shape = (LEVELS, GRIDS, PROCS, TILE, TILE)
    row_ids = lax.broadcasted_iota(jnp.int32, (TILE, TILE), 0)
    col_ids = lax.broadcasted_iota(jnp.int32, (TILE, TILE), 1)
    lower_mask = (row_ids > col_ids).astype(jnp.float32)
    diagonal_mask = (row_ids == col_ids).astype(jnp.float32)
    off_part = jax.random.normal(first_key, full_shape, jnp.float32) * (0.5 / math.sqrt(TILE))
    diag_part = jax.random.uniform(second_key, full_shape[:-1], jnp.float32, 0.6, 1.2)
    return off_part * lower_mask + diagonal_mask * diag_part[..., None]


def block_levels(stream_key, shape, cuts, smallest, high):
    def one(dim, parts):
        steps = jax.random.uniform(jax.random.fold_in(jax.random.fold_in(stream_key, 6), dim), (parts,), jnp.float32, smallest / len(cuts), high / len(cuts))
        return jnp.repeat(jnp.exp(steps), shape[dim] // parts).reshape((-1,) + (1,) * (len(shape) - dim - 1))

    gain = one(*cuts[0])
    for cut in cuts[1:]:
        gain = gain * one(*cut)
    return gain


def noise(key, extent, spread, reach, pieces=(), kind=jnp.bfloat16):
    result = spread * jax.random.normal(key, extent, jnp.float32)
    if pieces:
        result = result * block_levels(key, extent, pieces, -0.22, 0.18)
    return jnp.clip(result, -reach, reach).astype(kind)


def setup_inputs(seed: int = 0) -> dict:
    splits = jax.random.split(jax.random.key(seed), 5)
    return {
        "rhs": noise(splits[0], (LEVELS, GRIDS, PROCS, TILE, RHS), 1.0, 6.0, ((1, 4), (2, 8)), jnp.float32),
        "tile_pairs": draw_tile_pairs(jax.random.fold_in(splits[4], 71), 0),
        "tiles": noise(splits[2], (TRANS, GRIDS, PROCS, CAP, TILE, TILE), (TILE * PROCS) ** -0.5, 0.125, ((1, 4), (2, 8))),
        "dinv": draw_dinv(jax.random.fold_in(splits[4], 71), 0),
    }


def device_sums(device_inputs, rounded):
    pairs, tile_set, grid_index = device_inputs
    labels = lax.broadcasted_iota(jnp.int32, (CAP, CAP), 1)
    onehot = (pairs[:, None] == labels).astype(jnp.float32)
    dense = jnp.einsum("sq,sij->qij", onehot, tile_set.astype(jnp.float32), precision=lax.Precision.HIGHEST)
    dense = dense.reshape(2, PROCS, TILE, TILE)
    blocks = lax.dynamic_index_in_dim(rounded, grid_index, 0, keepdims=False).astype(jnp.float32)
    return jnp.einsum("dkij,kjr->dir", dense, blocks, precision=lax.Precision.HIGHEST)


def solve_blocks(factors, values):
    return jnp.einsum("gpij,gpjr->gpir", factors, values, precision=lax.Precision.HIGHEST)


def reference(rhs, tile_pairs, tiles, dinv):
    current = solve_blocks(dinv[0], rhs[0])
    solved = [current]
    owners = (jnp.arange(GRIDS * PROCS, dtype=jnp.int32) // PROCS).astype(jnp.int32)
    for height in range(1, LEVELS):
        rounded = current.astype(jnp.bfloat16)
        inputs = (tile_pairs[height - 1].reshape(GRIDS * PROCS, CAP),
                  tiles[height - 1].reshape(GRIDS * PROCS, CAP, TILE, TILE),
                  owners)
        partial_value = lax.map(lambda device_inputs: device_sums(device_inputs, rounded), inputs)
        partial_value = partial_value.reshape(GRIDS, PROCS, 2, TILE, RHS)
        partner_rows = np.arange(GRIDS) ^ (1 << (height - 1))
        update = partial_value[:, :, 0] + partial_value[partner_rows, :, 1]
        current = solve_blocks(dinv[height], rhs[height] - update)
        solved.append(current)
    return jnp.stack(solved)
```

```python
import functools

import jax
import jax.numpy as jnp
from jax import lax
from jax.experimental import pallas as pl
from jax.experimental.pallas import tpu as pltpu
from jax.sharding import PartitionSpec as P

MESH = pl.DeviceIdType.MESH
CHUNKS = 4


def flip(index, bit):
    return index + bit * (1 - 2 * lax.rem(lax.div(index, bit), 2))


def kernel(procs, chunks, rhs_hbm, pairs, tiles_hbm, dinv_hbm, out_hbm,
           rhs_v, tiles_v, dinv_v, out_v, table, held, near, away, come,
           in_sem, out_sem, send_sem, recv_sem, away_sem, come_sem):
    levels, rows, columns = rhs_v.shape
    trans, slots = tiles_v.shape[:2]
    width = columns // chunks
    half = rows // 2
    depth = procs // 2
    grid = lax.axis_index("grid")
    me = lax.axis_index("proc")
    y, z = lax.rem(me, 2), lax.div(me, 2)
    across = me + 1 - 2 * y
    twin_z = flip(z, 1)
    twin = twin_z * 2 + y
    partners = [flip(grid, 1 << t) for t in range(trans)]

    loads = []
    for level in range(levels):
        loads.append((
            pltpu.make_async_copy(dinv_hbm.at[level], dinv_v.at[level], in_sem.at[level, 0]),
            pltpu.make_async_copy(rhs_hbm.at[level], rhs_v.at[level], in_sem.at[level, 1]),
        ))
    tile_loads = [
        pltpu.make_async_copy(tiles_hbm.at[t], tiles_v.at[t], in_sem.at[t, 2]) for t in range(trans)
    ]
    for copy in loads[0]:
        copy.start()

    barrier = pltpu.get_barrier_semaphore()

    def greet(device):
        pl.semaphore_signal(barrier, inc=1, device_id=device, device_id_type=MESH)

    greet({"proc": across})
    for partner in partners:
        greet({"grid": partner})
    pl.when(z > 0)(lambda: greet({"proc": me - 2}))
    pl.when(z < depth - 1)(lambda: greet({"proc": me + 2}))

    for copy in tile_loads[:1] + list(loads[1]) + tile_loads[1:]:
        copy.start()
    for level in range(2, levels):
        for copy in loads[level]:
            copy.start()

    def cols(c):
        return pl.ds(pl.multiple_of(c * width, width), width)

    def send(t, c, block, way, target, part=None):
        src = held.at[t, c, block]
        slot = 0
        if part is not None:
            src = held.at[t, c, block, pl.ds(part * half, half)]
            slot = part
        return pltpu.make_async_remote_copy(
            src_ref=src, dst_ref=src,
            send_sem=send_sem.at[t, c, block, way],
            recv_sem=recv_sem.at[t, c, block, slot],
            device_id={"proc": target}, device_id_type=MESH,
        )

    def arrive(t, c, block, part=None):
        send(t, c, block, 0, across, part).wait_recv()

    def own(t, c, act):
        act(send(t, c, me, 2, across))
        pl.when(z > 0)(lambda: act(send(t, c, me, 0, me - 2)))
        pl.when(z < depth - 1)(lambda: act(send(t, c, me, 1, me + 2)))

    def relay(t, c, act, wait):
        for d in range(1, depth):
            for side in (1, -1):
                block = me + 2 * d * side

                def there(block=block, d=d, side=side):
                    if wait:
                        arrive(t, c, block)
                    if side == 1:
                        pl.when(z > 0)(lambda: act(send(t, c, block, 0, me - 2)))
                    else:
                        pl.when(z < depth - 1)(lambda: act(send(t, c, block, 1, me + 2)))
                    if d == 1:
                        mine = block == twin
                        pl.when(mine)(lambda: act(send(t, c, block, 2, across, 1)))
                        pl.when(jnp.logical_not(mine))(lambda: act(send(t, c, block, 2, across)))
                    else:
                        act(send(t, c, block, 2, across))

                pl.when((z + d < depth) if side == 1 else (z >= d))(there)
            if d == 1:
                if wait:
                    arrive(t, c, across)
                act(send(t, c, across, 0, twin, 0))

    def settle(t, c):
        for d in range(1, depth):
            for side in (1, -1):
                block = across + 2 * d * side

                def there(block=block, d=d):
                    if d == 1:
                        mine = lax.div(block, 2) == twin_z

                        @pl.when(mine)
                        def _():
                            arrive(t, c, block, 0)
                            arrive(t, c, block, 1)

                        pl.when(jnp.logical_not(mine))(lambda: arrive(t, c, block))
                    else:
                        arrive(t, c, block)

                pl.when((z + d < depth) if side == 1 else (z >= d))(there)

    def keep(level, c, value):
        out_v[level, :, cols(c)] = value
        store(level, c).start()

    def store(level, c):
        return pltpu.make_async_copy(
            out_v.at[level, :, cols(c)], out_hbm.at[level, :, cols(c)], out_sem.at[level, c]
        )

    def solve(level, c, values):
        return jnp.dot(dinv_v[level], values, precision=lax.Precision.HIGHEST,
                       preferred_element_type=jnp.float32)

    def first(c):
        value = solve(0, c, rhs_v[0, :, cols(c)])
        keep(0, c, value)
        held[0, c, me] = value.astype(held.dtype)

    def exchange(t, c):
        return pltpu.make_async_remote_copy(
            src_ref=away.at[t, c], dst_ref=come.at[t, c],
            send_sem=away_sem.at[t, c], recv_sem=come_sem.at[t, c],
            device_id={"grid": partners[t]}, device_id_type=MESH,
        )

    def multiply(t, c):
        blocks = held[t, c].reshape(procs * rows, width)
        away[t, c] = jnp.dot(table[t, 1], blocks, preferred_element_type=jnp.float32)
        exchange(t, c).start()
        near[t, c] = jnp.dot(table[t, 0], blocks, preferred_element_type=jnp.float32)

    def update(t, c):
        exchange(t, c).wait_recv()
        total = near[t, c] + come[t, c]
        value = solve(t + 1, c, rhs_v[t + 1, :, cols(c)] - total)
        keep(t + 1, c, value)
        if t + 1 < trans:
            held[t + 1, c, me] = value.astype(held.dtype)
            own(t + 1, c, lambda copy: copy.start())

    def build(t):
        for copy in (tile_loads if t == 0 else []) + list(loads[t + 1]):
            copy.wait()
        for d in range(2):
            def fill(k, _, d=d):
                slot = jnp.int32(0)
                found = jnp.int32(0)
                for s in range(slots):
                    hit = pairs[t, s] == d * procs + k
                    slot = jnp.where(hit, s, slot)
                    found = jnp.where(hit, 1, found)
                tile = tiles_v[t, slot].astype(jnp.float32) * found.astype(jnp.float32)
                table[t, d, :, pl.ds(pl.multiple_of(k * rows, rows), rows)] = tile.astype(table.dtype)
                return 0
            lax.fori_loop(0, procs, fill, 0)

    def each(lower, upper, step):
        def run(c, _):
            step(c)
            return 0
        lax.fori_loop(lower, upper, run, 0)

    for copy in loads[0]:
        copy.wait()
    first(0)
    pl.semaphore_wait(
        barrier,
        1 + trans + (z > 0).astype(jnp.int32) + (z < depth - 1).astype(jnp.int32),
    )
    own(0, 0, lambda copy: copy.start())

    @functools.partial(each, 1, chunks)
    def _(c):
        first(c)
        own(0, c, lambda copy: copy.start())

    build(0)
    for t in range(trans):
        relay(t, 0, lambda copy: copy.start(), True)
        if t > 0:
            update(t - 1, chunks - 1)
        settle(t, 0)
        multiply(t, 0)
        if t + 1 < trans:
            build(t + 1)

        @functools.partial(each, 1, chunks)
        def _(c):
            relay(t, c, lambda copy: copy.start(), True)
            update(t, c - 1)
            settle(t, c)
            multiply(t, c)

    update(trans - 1, chunks - 1)

    @functools.partial(each, 0, chunks)
    def _(c):
        for t in range(trans):
            own(t, c, lambda copy: copy.wait_send())
            relay(t, c, lambda copy: copy.wait_send(), False)
            exchange(t, c).wait_send()
        for level in range(levels):
            store(level, c).wait()


def body(rhs, tile_pairs, tiles, dinv):
    rhs_block, pairs = rhs[:, 0, 0], tile_pairs[:, 0, 0]
    tile_block, dinv_block = tiles[:, 0, 0], dinv[:, 0, 0]
    procs = lax.axis_size("proc")
    levels, rows, columns = rhs_block.shape
    trans, slots = pairs.shape
    chunks = CHUNKS
    width = columns // chunks
    any_spec = pl.BlockSpec(memory_space=pl.ANY)
    flops = 2 * rows * rows * columns * (levels * 6 + trans * 2 * procs)
    solved = pl.pallas_call(
        functools.partial(kernel, procs, chunks),
        out_shape=jax.ShapeDtypeStruct(rhs_block.shape, jnp.float32),
        in_specs=[any_spec, pl.BlockSpec(memory_space=pltpu.SMEM), any_spec, any_spec],
        out_specs=any_spec,
        scratch_shapes=[
            pltpu.VMEM((levels, rows, columns), jnp.float32),
            pltpu.VMEM((trans, slots, rows, rows), jnp.bfloat16),
            pltpu.VMEM((levels, rows, rows), jnp.float32),
            pltpu.VMEM((levels, rows, columns), jnp.float32),
            pltpu.VMEM((trans, 2, rows, procs * rows), jnp.bfloat16),
            pltpu.VMEM((trans, chunks, procs, rows, width), jnp.bfloat16),
            pltpu.VMEM((trans, chunks, rows, width), jnp.float32),
            pltpu.VMEM((trans, chunks, rows, width), jnp.float32),
            pltpu.VMEM((trans, chunks, rows, width), jnp.float32),
            pltpu.SemaphoreType.DMA((levels, 3)),
            pltpu.SemaphoreType.DMA((levels, chunks)),
            pltpu.SemaphoreType.DMA((trans, chunks, procs, 3)),
            pltpu.SemaphoreType.DMA((trans, chunks, procs, 2)),
            pltpu.SemaphoreType.DMA((trans, chunks)),
            pltpu.SemaphoreType.DMA((trans, chunks)),
        ],
        compiler_params=pltpu.CompilerParams(
            collective_id=0, has_side_effects=True, vmem_limit_bytes=60 * 1024 * 1024
        ),
        cost_estimate=pl.CostEstimate(
            flops=flops, bytes_accessed=14 * 1024 * 1024, transcendentals=0
        ),
    )(rhs_block, pairs, tile_block, dinv_block)
    return solved[:, None, None]


def solution(mesh):
    return jax.shard_map(
        body,
        mesh=mesh,
        in_specs=(
            P(None, "grid", "proc", None, None),
            P(None, "grid", "proc", None),
            P(None, "grid", "proc", None, None, None),
            P(None, "grid", "proc", None, None),
        ),
        out_specs=P(None, "grid", "proc", None, None),
        check_vma=False,
    )
```

```python
import functools

import jax
import jax.numpy as jnp
from jax import lax
from jax.experimental import pallas as pl
from jax.experimental.pallas import tpu as pltpu
from jax.sharding import PartitionSpec as P

MESH = pl.DeviceIdType.MESH
CHUNKS = 4
LEAD = 2


def flip(index, bit):
    return index + bit * (1 - 2 * lax.rem(lax.div(index, bit), 2))


def kernel(procs, chunks, rhs_hbm, pairs, tiles_hbm, dinv_hbm, out_hbm,
           rhs_v, tiles_v, dinv_v, out_v, table, held, near, away, come,
           in_sem, out_sem, send_sem, recv_sem, away_sem, come_sem):
    levels, rows, columns = rhs_v.shape
    trans, slots = tiles_v.shape[:2]
    width = columns // chunks
    half = rows // 2
    depth = procs // 2
    grid = lax.axis_index("grid")
    me = lax.axis_index("proc")
    y, z = lax.rem(me, 2), lax.div(me, 2)
    across = me + 1 - 2 * y
    twin_z = flip(z, 1)
    twin = twin_z * 2 + y
    partners = [flip(grid, 1 << t) for t in range(trans)]

    loads = []
    for level in range(levels):
        loads.append((
            pltpu.make_async_copy(dinv_hbm.at[level], dinv_v.at[level], in_sem.at[level, 0]),
            pltpu.make_async_copy(rhs_hbm.at[level], rhs_v.at[level], in_sem.at[level, 1]),
        ))
    tile_loads = [
        pltpu.make_async_copy(tiles_hbm.at[t], tiles_v.at[t], in_sem.at[t, 2]) for t in range(trans)
    ]
    for copy in loads[0]:
        copy.start()

    barrier = pltpu.get_barrier_semaphore()

    def greet(device):
        pl.semaphore_signal(barrier, inc=1, device_id=device, device_id_type=MESH)

    greet({"proc": across})
    for partner in partners:
        greet({"grid": partner})
    pl.when(z > 0)(lambda: greet({"proc": me - 2}))
    pl.when(z < depth - 1)(lambda: greet({"proc": me + 2}))

    for copy in tile_loads[:1] + list(loads[1]) + tile_loads[1:]:
        copy.start()
    for level in range(2, levels):
        for copy in loads[level]:
            copy.start()

    def cols(c):
        return pl.ds(pl.multiple_of(c * width, width), width)

    def send(t, c, block, way, target, part=None):
        src = held.at[t, c, block]
        slot = 0
        if part is not None:
            src = held.at[t, c, block, pl.ds(part * half, half)]
            slot = part
        return pltpu.make_async_remote_copy(
            src_ref=src, dst_ref=src,
            send_sem=send_sem.at[t, c, block, way],
            recv_sem=recv_sem.at[t, c, block, slot],
            device_id={"proc": target}, device_id_type=MESH,
        )

    def arrive(t, c, block, part=None):
        send(t, c, block, 0, across, part).wait_recv()

    def own(t, c, act):
        act(send(t, c, me, 2, across))
        pl.when(z > 0)(lambda: act(send(t, c, me, 0, me - 2)))
        pl.when(z < depth - 1)(lambda: act(send(t, c, me, 1, me + 2)))

    def hop(t, c, d, act, wait):
        for side in (1, -1):
            block = me + 2 * d * side

            def there(block=block, side=side):
                if wait:
                    arrive(t, c, block)
                if side == 1:
                    pl.when(z > 0)(lambda: act(send(t, c, block, 0, me - 2)))
                else:
                    pl.when(z < depth - 1)(lambda: act(send(t, c, block, 1, me + 2)))
                if d == 1:
                    mine = block == twin
                    pl.when(mine)(lambda: act(send(t, c, block, 2, across, 1)))
                    pl.when(jnp.logical_not(mine))(lambda: act(send(t, c, block, 2, across)))
                else:
                    act(send(t, c, block, 2, across))

            pl.when((z + d < depth) if side == 1 else (z >= d))(there)
        if d == 1:
            if wait:
                arrive(t, c, across)
            act(send(t, c, across, 0, twin, 0))

    def settle(t, c):
        for d in range(1, depth):
            for side in (1, -1):
                block = across + 2 * d * side

                def there(block=block, d=d):
                    if d == 1:
                        mine = lax.div(block, 2) == twin_z

                        @pl.when(mine)
                        def _():
                            arrive(t, c, block, 0)
                            arrive(t, c, block, 1)

                        pl.when(jnp.logical_not(mine))(lambda: arrive(t, c, block))
                    else:
                        arrive(t, c, block)

                pl.when((z + d < depth) if side == 1 else (z >= d))(there)

    def keep(level, c, value):
        out_v[level, :, cols(c)] = value
        store(level, c).start()

    def store(level, c):
        return pltpu.make_async_copy(
            out_v.at[level, :, cols(c)], out_hbm.at[level, :, cols(c)], out_sem.at[level, c]
        )

    def solve(level, c, values):
        return jnp.dot(dinv_v[level], values, precision=lax.Precision.HIGHEST,
                       preferred_element_type=jnp.float32)

    def first(c):
        value = solve(0, c, rhs_v[0, :, cols(c)])
        keep(0, c, value)
        held[0, c, me] = value.astype(held.dtype)

    def exchange(t, c):
        return pltpu.make_async_remote_copy(
            src_ref=away.at[t, c], dst_ref=come.at[t, c],
            send_sem=away_sem.at[t, c], recv_sem=come_sem.at[t, c],
            device_id={"grid": partners[t]}, device_id_type=MESH,
        )

    def multiply(t, c):
        blocks = held[t, c].reshape(procs * rows, width)
        away[t, c] = jnp.dot(table[t, 1], blocks, preferred_element_type=jnp.float32)
        exchange(t, c).start()
        near[t, c] = jnp.dot(table[t, 0], blocks, preferred_element_type=jnp.float32)

    def update(t, c):
        exchange(t, c).wait_recv()
        total = near[t, c] + come[t, c]
        value = solve(t + 1, c, rhs_v[t + 1, :, cols(c)] - total)
        keep(t + 1, c, value)
        if t + 1 < trans:
            held[t + 1, c, me] = value.astype(held.dtype)
            own(t + 1, c, lambda copy: copy.start())

    def build(t):
        for copy in (tile_loads if t == 0 else []) + list(loads[t + 1]):
            copy.wait()
        for d in range(2):
            def fill(k, _, d=d):
                slot = jnp.int32(0)
                found = jnp.int32(0)
                for s in range(slots):
                    hit = pairs[t, s] == d * procs + k
                    slot = jnp.where(hit, s, slot)
                    found = jnp.where(hit, 1, found)
                tile = tiles_v[t, slot].astype(jnp.float32) * found.astype(jnp.float32)
                table[t, d, :, pl.ds(pl.multiple_of(k * rows, rows), rows)] = tile.astype(table.dtype)
                return 0
            lax.fori_loop(0, procs, fill, 0)

    def each(lower, upper, step):
        def run(c, _):
            step(c)
            return 0
        lax.fori_loop(lower, upper, run, 0)

    for copy in loads[0]:
        copy.wait()
    first(0)
    pl.semaphore_wait(
        barrier,
        1 + trans + (z > 0).astype(jnp.int32) + (z < depth - 1).astype(jnp.int32),
    )
    own(0, 0, lambda copy: copy.start())
    lead = min(LEAD, chunks)

    @functools.partial(each, 1, lead)
    def _(c):
        first(c)
        own(0, c, lambda copy: copy.start())

    build(0)
    stride = max(chunks, depth + 2)

    @functools.partial(each, 0, (trans - 1) * stride + chunks + depth)
    def _(tick):
        def at(lag, step):
            for t in range(trans):
                c = tick - lag - t * stride
                pl.when(jnp.logical_and(c >= 0, c < chunks))(functools.partial(step, t, c))

        for d in range(depth - 1, 0, -1):
            for t in range(trans):
                c = tick - (d - 1) - t * stride
                pl.when(jnp.logical_and(c >= 0, c < chunks))(
                    functools.partial(hop, t, c, d, lambda copy: copy.start(), True))

        @pl.when(tick + lead < chunks)
        def _():
            first(tick + lead)
            own(0, tick + lead, lambda copy: copy.start())

        at(depth, update)

        def gathered(t, c):
            settle(t, c)
            multiply(t, c)

        at(depth - 1, gathered)
        for t in range(1, trans):
            pl.when(tick == t * stride)(functools.partial(build, t))

    @functools.partial(each, 0, chunks)
    def _(c):
        for t in range(trans):
            own(t, c, lambda copy: copy.wait_send())
            for d in range(1, depth):
                hop(t, c, d, lambda copy: copy.wait_send(), False)
            exchange(t, c).wait_send()
        for level in range(levels):
            store(level, c).wait()


def body(rhs, tile_pairs, tiles, dinv):
    rhs_block, pairs = rhs[:, 0, 0], tile_pairs[:, 0, 0]
    tile_block, dinv_block = tiles[:, 0, 0], dinv[:, 0, 0]
    procs = lax.axis_size("proc")
    levels, rows, columns = rhs_block.shape
    trans, slots = pairs.shape
    chunks = CHUNKS
    width = columns // chunks
    any_spec = pl.BlockSpec(memory_space=pl.ANY)
    flops = 2 * rows * rows * columns * (levels * 6 + trans * 2 * procs)
    solved = pl.pallas_call(
        functools.partial(kernel, procs, chunks),
        out_shape=jax.ShapeDtypeStruct(rhs_block.shape, jnp.float32),
        in_specs=[any_spec, pl.BlockSpec(memory_space=pltpu.SMEM), any_spec, any_spec],
        out_specs=any_spec,
        scratch_shapes=[
            pltpu.VMEM((levels, rows, columns), jnp.float32),
            pltpu.VMEM((trans, slots, rows, rows), jnp.bfloat16),
            pltpu.VMEM((levels, rows, rows), jnp.float32),
            pltpu.VMEM((levels, rows, columns), jnp.float32),
            pltpu.VMEM((trans, 2, rows, procs * rows), jnp.bfloat16),
            pltpu.VMEM((trans, chunks, procs, rows, width), jnp.bfloat16),
            pltpu.VMEM((trans, chunks, rows, width), jnp.float32),
            pltpu.VMEM((trans, chunks, rows, width), jnp.float32),
            pltpu.VMEM((trans, chunks, rows, width), jnp.float32),
            pltpu.SemaphoreType.DMA((levels, 3)),
            pltpu.SemaphoreType.DMA((levels, chunks)),
            pltpu.SemaphoreType.DMA((trans, chunks, procs, 3)),
            pltpu.SemaphoreType.DMA((trans, chunks, procs, 2)),
            pltpu.SemaphoreType.DMA((trans, chunks)),
            pltpu.SemaphoreType.DMA((trans, chunks)),
        ],
        compiler_params=pltpu.CompilerParams(
            collective_id=0, has_side_effects=True, vmem_limit_bytes=60 * 1024 * 1024
        ),
        cost_estimate=pl.CostEstimate(
            flops=flops, bytes_accessed=14 * 1024 * 1024, transcendentals=0
        ),
    )(rhs_block, pairs, tile_block, dinv_block)
    return solved[:, None, None]


def solution(mesh):
    return jax.shard_map(
        body,
        mesh=mesh,
        in_specs=(
            P(None, "grid", "proc", None, None),
            P(None, "grid", "proc", None),
            P(None, "grid", "proc", None, None, None),
            P(None, "grid", "proc", None, None),
        ),
        out_specs=P(None, "grid", "proc", None, None),
        check_vma=False,
    )
```

```python
import functools

import jax
import jax.numpy as jnp
from jax import lax
from jax.experimental import pallas as pl
from jax.experimental.pallas import tpu as pltpu
from jax.sharding import PartitionSpec as P

MESH = pl.DeviceIdType.MESH
CHUNKS = 8
LEAD = 3


def flip(index, bit):
    return index + bit * (1 - 2 * lax.rem(lax.div(index, bit), 2))


def kernel(procs, chunks, rhs_hbm, pairs, tiles_hbm, dinv_hbm, out_hbm,
           rhs_v, tiles_v, dinv_v, out_v, table, held, near, away, come,
           in_sem, out_sem, send_sem, recv_sem, away_sem, come_sem):
    levels, rows, columns = rhs_v.shape
    trans, slots = tiles_v.shape[:2]
    width = columns // chunks
    half = rows // 2
    depth = procs // 2
    grid = lax.axis_index("grid")
    me = lax.axis_index("proc")
    y, z = lax.rem(me, 2), lax.div(me, 2)
    across = me + 1 - 2 * y
    twin_z = flip(z, 1)
    twin = twin_z * 2 + y
    partners = [flip(grid, 1 << t) for t in range(trans)]

    loads = []
    for level in range(levels):
        loads.append((
            pltpu.make_async_copy(dinv_hbm.at[level], dinv_v.at[level], in_sem.at[level, 0]),
            pltpu.make_async_copy(rhs_hbm.at[level], rhs_v.at[level], in_sem.at[level, 1]),
        ))
    tile_loads = [
        pltpu.make_async_copy(tiles_hbm.at[t], tiles_v.at[t], in_sem.at[t, 2]) for t in range(trans)
    ]
    for copy in loads[0]:
        copy.start()

    barrier = pltpu.get_barrier_semaphore()

    def greet(device):
        pl.semaphore_signal(barrier, inc=1, device_id=device, device_id_type=MESH)

    greet({"proc": across})
    for partner in partners:
        greet({"grid": partner})
    pl.when(z > 0)(lambda: greet({"proc": me - 2}))
    pl.when(z < depth - 1)(lambda: greet({"proc": me + 2}))

    for copy in tile_loads[:1] + list(loads[1]) + tile_loads[1:]:
        copy.start()
    for level in range(2, levels):
        for copy in loads[level]:
            copy.start()

    def cols(c):
        return pl.ds(pl.multiple_of(c * width, width), width)

    def send(t, c, block, way, target, part=None):
        src = held.at[t, c, block]
        slot = 0
        if part is not None:
            src = held.at[t, c, block, pl.ds(part * half, half)]
            slot = part
        return pltpu.make_async_remote_copy(
            src_ref=src, dst_ref=src,
            send_sem=send_sem.at[t, c, block, way],
            recv_sem=recv_sem.at[t, c, block, slot],
            device_id={"proc": target}, device_id_type=MESH,
        )

    def arrive(t, c, block, part=None):
        send(t, c, block, 0, across, part).wait_recv()

    def own(t, c, act):
        act(send(t, c, me, 2, across))
        pl.when(z > 0)(lambda: act(send(t, c, me, 0, me - 2)))
        pl.when(z < depth - 1)(lambda: act(send(t, c, me, 1, me + 2)))

    def hop(t, c, d, act, wait):
        for side in (1, -1):
            block = me + 2 * d * side

            def there(block=block, side=side):
                if wait:
                    arrive(t, c, block)
                if side == 1:
                    pl.when(z > 0)(lambda: act(send(t, c, block, 0, me - 2)))
                else:
                    pl.when(z < depth - 1)(lambda: act(send(t, c, block, 1, me + 2)))
                if d == 1:
                    mine = block == twin
                    pl.when(mine)(lambda: act(send(t, c, block, 2, across, 1)))
                    pl.when(jnp.logical_not(mine))(lambda: act(send(t, c, block, 2, across)))
                else:
                    act(send(t, c, block, 2, across))

            pl.when((z + d < depth) if side == 1 else (z >= d))(there)
        if d == 1:
            if wait:
                arrive(t, c, across)
            act(send(t, c, across, 0, twin, 0))

    def settle(t, c):
        for d in range(1, depth):
            for side in (1, -1):
                block = across + 2 * d * side

                def there(block=block, d=d):
                    if d == 1:
                        mine = lax.div(block, 2) == twin_z

                        @pl.when(mine)
                        def _():
                            arrive(t, c, block, 0)
                            arrive(t, c, block, 1)

                        pl.when(jnp.logical_not(mine))(lambda: arrive(t, c, block))
                    else:
                        arrive(t, c, block)

                pl.when((z + d < depth) if side == 1 else (z >= d))(there)

    def keep(level, c, value):
        out_v[level, :, cols(c)] = value
        store(level, c).start()

    def store(level, c):
        return pltpu.make_async_copy(
            out_v.at[level, :, cols(c)], out_hbm.at[level, :, cols(c)], out_sem.at[level, c]
        )

    def solve(level, c, values):
        return jnp.dot(dinv_v[level], values, precision=lax.Precision.HIGHEST,
                       preferred_element_type=jnp.float32)

    def first(c):
        value = solve(0, c, rhs_v[0, :, cols(c)])
        keep(0, c, value)
        held[0, c, me] = value.astype(held.dtype)

    def exchange(t, c):
        return pltpu.make_async_remote_copy(
            src_ref=away.at[t, c], dst_ref=come.at[t, c],
            send_sem=away_sem.at[t, c], recv_sem=come_sem.at[t, c],
            device_id={"grid": partners[t]}, device_id_type=MESH,
        )

    def multiply(t, c):
        blocks = held[t, c].reshape(procs * rows, width)
        away[t, c] = jnp.dot(table[t, 1], blocks, preferred_element_type=jnp.float32)
        exchange(t, c).start()
        near[t, c] = jnp.dot(table[t, 0], blocks, preferred_element_type=jnp.float32)

    def update(t, c):
        exchange(t, c).wait_recv()
        total = near[t, c] + come[t, c]
        value = solve(t + 1, c, rhs_v[t + 1, :, cols(c)] - total)
        keep(t + 1, c, value)
        if t + 1 < trans:
            held[t + 1, c, me] = value.astype(held.dtype)
            own(t + 1, c, lambda copy: copy.start())

    def build(t):
        for copy in (tile_loads if t == 0 else []) + list(loads[t + 1]):
            copy.wait()
        for d in range(2):
            def fill(k, _, d=d):
                slot = jnp.int32(0)
                found = jnp.int32(0)
                for s in range(slots):
                    hit = pairs[t, s] == d * procs + k
                    slot = jnp.where(hit, s, slot)
                    found = jnp.where(hit, 1, found)
                tile = tiles_v[t, slot].astype(jnp.float32) * found.astype(jnp.float32)
                table[t, d, :, pl.ds(pl.multiple_of(k * rows, rows), rows)] = tile.astype(table.dtype)
                return 0
            lax.fori_loop(0, procs, fill, 0)

    def each(lower, upper, step):
        def run(c, _):
            step(c)
            return 0
        lax.fori_loop(lower, upper, run, 0)

    for copy in loads[0]:
        copy.wait()
    first(0)
    pl.semaphore_wait(
        barrier,
        1 + trans + (z > 0).astype(jnp.int32) + (z < depth - 1).astype(jnp.int32),
    )
    own(0, 0, lambda copy: copy.start())
    lead = min(LEAD, chunks)

    @functools.partial(each, 1, lead)
    def _(c):
        first(c)
        own(0, c, lambda copy: copy.start())

    build(0)
    stride = max(chunks, depth + 2)

    @functools.partial(each, 0, (trans - 1) * stride + chunks + depth)
    def _(tick):
        def at(lag, step):
            for t in range(trans):
                c = tick - lag - t * stride
                pl.when(jnp.logical_and(c >= 0, c < chunks))(functools.partial(step, t, c))

        for d in range(depth - 1, 0, -1):
            for t in range(trans):
                c = tick - (d - 1) - t * stride
                pl.when(jnp.logical_and(c >= 0, c < chunks))(
                    functools.partial(hop, t, c, d, lambda copy: copy.start(), True))

        @pl.when(tick + lead < chunks)
        def _():
            first(tick + lead)
            own(0, tick + lead, lambda copy: copy.start())

        at(depth, update)

        def gathered(t, c):
            settle(t, c)
            multiply(t, c)

        at(depth - 1, gathered)
        for t in range(1, trans):
            pl.when(tick == t * stride)(functools.partial(build, t))

    @functools.partial(each, 0, chunks)
    def _(c):
        for t in range(trans):
            own(t, c, lambda copy: copy.wait_send())
            for d in range(1, depth):
                hop(t, c, d, lambda copy: copy.wait_send(), False)
            exchange(t, c).wait_send()
        for level in range(levels):
            store(level, c).wait()


def body(rhs, tile_pairs, tiles, dinv):
    rhs_block, pairs = rhs[:, 0, 0], tile_pairs[:, 0, 0]
    tile_block, dinv_block = tiles[:, 0, 0], dinv[:, 0, 0]
    procs = lax.axis_size("proc")
    levels, rows, columns = rhs_block.shape
    trans, slots = pairs.shape
    chunks = CHUNKS
    width = columns // chunks
    any_spec = pl.BlockSpec(memory_space=pl.ANY)
    flops = 2 * rows * rows * columns * (levels * 6 + trans * 2 * procs)
    solved = pl.pallas_call(
        functools.partial(kernel, procs, chunks),
        out_shape=jax.ShapeDtypeStruct(rhs_block.shape, jnp.float32),
        in_specs=[any_spec, pl.BlockSpec(memory_space=pltpu.SMEM), any_spec, any_spec],
        out_specs=any_spec,
        scratch_shapes=[
            pltpu.VMEM((levels, rows, columns), jnp.float32),
            pltpu.VMEM((trans, slots, rows, rows), jnp.bfloat16),
            pltpu.VMEM((levels, rows, rows), jnp.float32),
            pltpu.VMEM((levels, rows, columns), jnp.float32),
            pltpu.VMEM((trans, 2, rows, procs * rows), jnp.bfloat16),
            pltpu.VMEM((trans, chunks, procs, rows, width), jnp.bfloat16),
            pltpu.VMEM((trans, chunks, rows, width), jnp.float32),
            pltpu.VMEM((trans, chunks, rows, width), jnp.float32),
            pltpu.VMEM((trans, chunks, rows, width), jnp.float32),
            pltpu.SemaphoreType.DMA((levels, 3)),
            pltpu.SemaphoreType.DMA((levels, chunks)),
            pltpu.SemaphoreType.DMA((trans, chunks, procs, 3)),
            pltpu.SemaphoreType.DMA((trans, chunks, procs, 2)),
            pltpu.SemaphoreType.DMA((trans, chunks)),
            pltpu.SemaphoreType.DMA((trans, chunks)),
        ],
        compiler_params=pltpu.CompilerParams(
            collective_id=0, has_side_effects=True, vmem_limit_bytes=60 * 1024 * 1024
        ),
        cost_estimate=pl.CostEstimate(
            flops=flops, bytes_accessed=14 * 1024 * 1024, transcendentals=0
        ),
    )(rhs_block, pairs, tile_block, dinv_block)
    return solved[:, None, None]


def solution(mesh):
    return jax.shard_map(
        body,
        mesh=mesh,
        in_specs=(
            P(None, "grid", "proc", None, None),
            P(None, "grid", "proc", None),
            P(None, "grid", "proc", None, None, None),
            P(None, "grid", "proc", None, None),
        ),
        out_specs=P(None, "grid", "proc", None, None),
        check_vma=False,
    )
```

```python
import functools

import jax
import jax.numpy as jnp
from jax import lax
from jax.experimental import pallas as pl
from jax.experimental.pallas import tpu as pltpu
from jax.sharding import PartitionSpec as P

MESH = pl.DeviceIdType.MESH
CHUNKS = 4
LEAD = 4


def flip(index, bit):
    return index + bit * (1 - 2 * lax.rem(lax.div(index, bit), 2))


def kernel(procs, chunks, rhs_hbm, pairs, tiles_hbm, dinv_hbm, out_hbm,
           rhs_v, tiles_v, dinv_v, out_v, table, held, near, away, come,
           in_sem, out_sem, send_sem, recv_sem, away_sem, come_sem):
    levels, rows, columns = rhs_v.shape
    trans, slots = tiles_v.shape[:2]
    width = columns // chunks
    half = rows // 2
    depth = procs // 2
    grid = lax.axis_index("grid")
    me = lax.axis_index("proc")
    y, z = lax.rem(me, 2), lax.div(me, 2)
    across = me + 1 - 2 * y
    twin_z = flip(z, 1)
    twin = twin_z * 2 + y
    partners = [flip(grid, 1 << t) for t in range(trans)]

    loads = []
    for level in range(levels):
        loads.append((
            pltpu.make_async_copy(dinv_hbm.at[level], dinv_v.at[level], in_sem.at[level, 0]),
            pltpu.make_async_copy(rhs_hbm.at[level], rhs_v.at[level], in_sem.at[level, 1]),
        ))
    tile_loads = [
        pltpu.make_async_copy(tiles_hbm.at[t], tiles_v.at[t], in_sem.at[t, 2]) for t in range(trans)
    ]
    for copy in loads[0]:
        copy.start()

    barrier = pltpu.get_barrier_semaphore()

    def greet(device):
        pl.semaphore_signal(barrier, inc=1, device_id=device, device_id_type=MESH)

    greet({"proc": across})
    for partner in partners:
        greet({"grid": partner})
    pl.when(z > 0)(lambda: greet({"proc": me - 2}))
    pl.when(z < depth - 1)(lambda: greet({"proc": me + 2}))

    for copy in tile_loads[:1] + list(loads[1]) + tile_loads[1:]:
        copy.start()
    for level in range(2, levels):
        for copy in loads[level]:
            copy.start()

    def cols(c):
        return pl.ds(pl.multiple_of(c * width, width), width)

    def send(t, c, block, way, target, part=None):
        src = held.at[t, c, block]
        slot = 0
        if part is not None:
            src = held.at[t, c, block, pl.ds(part * half, half)]
            slot = part
        return pltpu.make_async_remote_copy(
            src_ref=src, dst_ref=src,
            send_sem=send_sem.at[t, c, block, way],
            recv_sem=recv_sem.at[t, c, block, slot],
            device_id={"proc": target}, device_id_type=MESH,
        )

    def arrive(t, c, block, part=None):
        send(t, c, block, 0, across, part).wait_recv()

    def own(t, c, act):
        act(send(t, c, me, 2, across))
        pl.when(z > 0)(lambda: act(send(t, c, me, 0, me - 2)))
        pl.when(z < depth - 1)(lambda: act(send(t, c, me, 1, me + 2)))

    def hop(t, c, d, act, wait):
        for side in (1, -1):
            block = me + 2 * d * side

            def there(block=block, side=side):
                if wait:
                    arrive(t, c, block)
                if side == 1:
                    pl.when(z > 0)(lambda: act(send(t, c, block, 0, me - 2)))
                else:
                    pl.when(z < depth - 1)(lambda: act(send(t, c, block, 1, me + 2)))
                if d == 1:
                    mine = block == twin
                    pl.when(mine)(lambda: act(send(t, c, block, 2, across, 1)))
                    pl.when(jnp.logical_not(mine))(lambda: act(send(t, c, block, 2, across)))
                else:
                    act(send(t, c, block, 2, across))

            pl.when((z + d < depth) if side == 1 else (z >= d))(there)
        if d == 1:
            if wait:
                arrive(t, c, across)
            act(send(t, c, across, 0, twin, 0))

    def settle(t, c):
        for d in range(1, depth):
            for side in (1, -1):
                block = across + 2 * d * side

                def there(block=block, d=d):
                    if d == 1:
                        mine = lax.div(block, 2) == twin_z

                        @pl.when(mine)
                        def _():
                            arrive(t, c, block, 0)
                            arrive(t, c, block, 1)

                        pl.when(jnp.logical_not(mine))(lambda: arrive(t, c, block))
                    else:
                        arrive(t, c, block)

                pl.when((z + d < depth) if side == 1 else (z >= d))(there)

    def keep(level, c, value):
        out_v[level, :, cols(c)] = value
        store(level, c).start()

    def store(level, c):
        return pltpu.make_async_copy(
            out_v.at[level, :, cols(c)], out_hbm.at[level, :, cols(c)], out_sem.at[level, c]
        )

    def solve(level, c, values):
        return jnp.dot(dinv_v[level], values, precision=lax.Precision.HIGHEST,
                       preferred_element_type=jnp.float32)

    def first(c):
        value = solve(0, c, rhs_v[0, :, cols(c)])
        keep(0, c, value)
        held[0, c, me] = value.astype(held.dtype)

    def exchange(t, c):
        return pltpu.make_async_remote_copy(
            src_ref=away.at[t, c], dst_ref=come.at[t, c],
            send_sem=away_sem.at[t, c], recv_sem=come_sem.at[t, c],
            device_id={"grid": partners[t]}, device_id_type=MESH,
        )

    def multiply(t, c):
        blocks = held[t, c].reshape(procs * rows, width)
        away[t, c] = jnp.dot(table[t, 1], blocks, preferred_element_type=jnp.float32)
        exchange(t, c).start()
        near[t, c] = jnp.dot(table[t, 0], blocks, preferred_element_type=jnp.float32)

    def update(t, c):
        exchange(t, c).wait_recv()
        total = near[t, c] + come[t, c]
        value = solve(t + 1, c, rhs_v[t + 1, :, cols(c)] - total)
        keep(t + 1, c, value)
        if t + 1 < trans:
            held[t + 1, c, me] = value.astype(held.dtype)
            own(t + 1, c, lambda copy: copy.start())

    def build(t):
        for copy in (tile_loads if t == 0 else []) + list(loads[t + 1]):
            copy.wait()
        for d in range(2):
            def fill(k, _, d=d):
                slot = jnp.int32(0)
                found = jnp.int32(0)
                for s in range(slots):
                    hit = pairs[t, s] == d * procs + k
                    slot = jnp.where(hit, s, slot)
                    found = jnp.where(hit, 1, found)
                tile = tiles_v[t, slot].astype(jnp.float32) * found.astype(jnp.float32)
                table[t, d, :, pl.ds(pl.multiple_of(k * rows, rows), rows)] = tile.astype(table.dtype)
                return 0
            lax.fori_loop(0, procs, fill, 0)

    def each(lower, upper, step):
        def run(c, _):
            step(c)
            return 0
        lax.fori_loop(lower, upper, run, 0)

    for copy in loads[0]:
        copy.wait()
    first(0)
    pl.semaphore_wait(
        barrier,
        1 + trans + (z > 0).astype(jnp.int32) + (z < depth - 1).astype(jnp.int32),
    )
    own(0, 0, lambda copy: copy.start())
    lead = min(LEAD, chunks)

    @functools.partial(each, 1, lead)
    def _(c):
        first(c)
        own(0, c, lambda copy: copy.start())

    for t in range(trans):
        build(t)
    stride = max(chunks, depth + 1)

    @functools.partial(each, 0, (trans - 1) * stride + chunks + depth)
    def _(tick):
        def at(lag, step):
            for t in range(trans):
                c = tick - lag - t * stride
                pl.when(jnp.logical_and(c >= 0, c < chunks))(functools.partial(step, t, c))

        for d in range(depth - 1, 0, -1):
            for t in range(trans):
                c = tick - (d - 1) - t * stride
                pl.when(jnp.logical_and(c >= 0, c < chunks))(
                    functools.partial(hop, t, c, d, lambda copy: copy.start(), True))

        @pl.when(tick + lead < chunks)
        def _():
            first(tick + lead)
            own(0, tick + lead, lambda copy: copy.start())

        at(depth, update)

        def gathered(t, c):
            settle(t, c)
            multiply(t, c)

        at(depth - 1, gathered)

    @functools.partial(each, 0, chunks)
    def _(c):
        for t in range(trans):
            own(t, c, lambda copy: copy.wait_send())
            for d in range(1, depth):
                hop(t, c, d, lambda copy: copy.wait_send(), False)
            exchange(t, c).wait_send()
        for level in range(levels):
            store(level, c).wait()


def body(rhs, tile_pairs, tiles, dinv):
    rhs_block, pairs = rhs[:, 0, 0], tile_pairs[:, 0, 0]
    tile_block, dinv_block = tiles[:, 0, 0], dinv[:, 0, 0]
    procs = lax.axis_size("proc")
    levels, rows, columns = rhs_block.shape
    trans, slots = pairs.shape
    chunks = CHUNKS
    width = columns // chunks
    any_spec = pl.BlockSpec(memory_space=pl.ANY)
    flops = 2 * rows * rows * columns * (levels * 6 + trans * 2 * procs)
    solved = pl.pallas_call(
        functools.partial(kernel, procs, chunks),
        out_shape=jax.ShapeDtypeStruct(rhs_block.shape, jnp.float32),
        in_specs=[any_spec, pl.BlockSpec(memory_space=pltpu.SMEM), any_spec, any_spec],
        out_specs=any_spec,
        scratch_shapes=[
            pltpu.VMEM((levels, rows, columns), jnp.float32),
            pltpu.VMEM((trans, slots, rows, rows), jnp.bfloat16),
            pltpu.VMEM((levels, rows, rows), jnp.float32),
            pltpu.VMEM((levels, rows, columns), jnp.float32),
            pltpu.VMEM((trans, 2, rows, procs * rows), jnp.bfloat16),
            pltpu.VMEM((trans, chunks, procs, rows, width), jnp.bfloat16),
            pltpu.VMEM((trans, chunks, rows, width), jnp.float32),
            pltpu.VMEM((trans, chunks, rows, width), jnp.float32),
            pltpu.VMEM((trans, chunks, rows, width), jnp.float32),
            pltpu.SemaphoreType.DMA((levels, 3)),
            pltpu.SemaphoreType.DMA((levels, chunks)),
            pltpu.SemaphoreType.DMA((trans, chunks, procs, 3)),
            pltpu.SemaphoreType.DMA((trans, chunks, procs, 2)),
            pltpu.SemaphoreType.DMA((trans, chunks)),
            pltpu.SemaphoreType.DMA((trans, chunks)),
        ],
        compiler_params=pltpu.CompilerParams(
            collective_id=0, has_side_effects=True, vmem_limit_bytes=60 * 1024 * 1024
        ),
        cost_estimate=pl.CostEstimate(
            flops=flops, bytes_accessed=14 * 1024 * 1024, transcendentals=0
        ),
    )(rhs_block, pairs, tile_block, dinv_block)
    return solved[:, None, None]


def solution(mesh):
    return jax.shard_map(
        body,
        mesh=mesh,
        in_specs=(
            P(None, "grid", "proc", None, None),
            P(None, "grid", "proc", None),
            P(None, "grid", "proc", None, None, None),
            P(None, "grid", "proc", None, None),
        ),
        out_specs=P(None, "grid", "proc", None, None),
        check_vma=False,
    )
```
